32 devices in a mesh: groups: 2 (over y), graph: 4 (over z), pipe: 2 (over x), feat: 2 (over core).
Axes of the slice: x: 2, y: 2, z: 4, core: 2. Of those that a mesh axis runs over, the one named last changes fastest.
Arguments:
- atom_state: bfloat16 [4, 32, 512], P(('groups', 'pipe'), 'graph'), parts along dimension 0, may hold values from -6 to 6
- direction: bfloat16 [4, 32, 512], P(('groups', 'pipe'), 'graph'), parts along dimension 0, may hold values from -6 to 6
- upstream: bfloat16 [4, 32, 512], P(('groups', 'pipe'), 'graph'), parts along dimension 0, may hold values from -6 to 6
- edge_state: bfloat16 [4, 2048, 512], P(('groups', 'pipe'), 'graph'), parts along dimension 0, may hold values from -6 to 6
- edge_src: int32 [4, 2048], P(('groups', 'pipe'), 'graph'), parts along dimension 0, may hold values from 0 to 31
- edge_tgt: int32 [4, 2048], P(('groups', 'pipe'), 'graph'), parts along dimension 0, may hold values from 0 to 31
- edge_blocks: int32 [4, 4], P(('groups', 'pipe'), 'graph'), parts along dimension 0, may hold values from 1 to 4, as said below
- trip_in: int32 [4, 1024], P(('groups', 'pipe'), 'graph'), parts along dimension 0, may hold values from 0 to 511, as said below
- trip_out: int32 [4, 1024], P(('groups', 'pipe'), 'graph'), parts along dimension 0, may hold values from 0 to 511, as said below
- trip_coef: bfloat16 [4, 1024], P(('groups', 'pipe'), 'graph'), parts along dimension 0, may hold values from -1 to 1
- w_src: bfloat16 [512, 512], replicated, may hold values from -0.25 to 0.25
- w_tgt: bfloat16 [512, 512], replicated, may hold values from -0.25 to 0.25
- w_in: bfloat16 [512, 1024], P(None, 'feat'), may hold values from -0.25 to 0.25
- w_out: bfloat16 [1024, 512], P('feat'), may hold values from -0.03125 to 0.03125
Outputs:
- atom_update: bfloat16 [4, 32, 512], P(('groups', 'pipe'), 'graph'), parts along dimension 0
- grad_state: float32 [4, 32, 512], P(('groups', 'pipe'), 'graph'), parts along dimension 0
- hvp_state: float32 [4, 32, 512], P(('groups', 'pipe'), 'graph'), parts along dimension 0
The draws below stay inside these ranges and needn't reach their ends.
There are 2 independent parts, one for each index of `groups`. The reference program is written for one: setup_inputs(seed, part) draws one part's arguments, and reference() takes and returns one part's arrays. A program takes and returns all parts, laid end to end along the dimension named above; an argument that names none is the same for every part. Nothing has to cross between parts.
Inputs may be any that keep to these rules, and one draw needn't show every extreme that they name: `edge_blocks`: number of leading blocks of 128 edge slots of one device that hold edges; the other slots of that device are padding, whatever ids they carry. In every micro-batch some device is full. `trip_in`: A slot of the same device that holds an edge. `trip_out`: A slot of the same device that holds an edge.
All inputs are finite; a program needn't handle non-finite values.
Results may differ from the reference program's by a relative error of at most 0.0049.
Values may be sent and summed in bfloat16 or wider, within the bound.
A program may use at most 64 MiB of HBM per device.

```python
import jax
import jax.numpy as jnp
from jax import lax

D = 512
HID = 1024
EBLOCK = 128
EDGE_DEV = 512
TRIP_DEV = 256
ATOMS = 32
EDGES = 2048
TRIPS = 1024
SHARDS = 4
MB = 2


def block_table(key):
    full_count = EDGE_DEV // EBLOCK
    raw_counts = jax.random.randint(jax.random.fold_in(key, 7), (MB, SHARDS), 1, full_count + 1)
    full_spot = jax.random.randint(jax.random.fold_in(key, 8), (MB, 1), 0, SHARDS)
    shard_iota = jnp.arange(SHARDS, dtype=jnp.int32)[None, :]
    return jnp.where(shard_iota == full_spot, full_count, raw_counts).astype(jnp.int32)


def trip_slots(key, own_constant):
    limits = block_table(key) * EBLOCK
    key = jax.random.fold_in(key, own_constant)
    raw_ids = jax.random.randint(jax.random.fold_in(key, 1), (MB, TRIPS), 0, 1 << 20)
    trip_owner = jnp.arange(TRIPS, dtype=jnp.int32) // TRIP_DEV
    bounds = limits[:, trip_owner]
    slot_ids = raw_ids % bounds
    top_spot = jax.random.randint(jax.random.fold_in(key, 2), (MB, SHARDS), 0, TRIP_DEV)
    local_iota = jnp.arange(TRIPS, dtype=jnp.int32) % TRIP_DEV
    slot_ids = jnp.where(local_iota[None, :] == top_spot[:, trip_owner], bounds - 1, slot_ids)
    return slot_ids.astype(jnp.int32)


def draw_edge_blocks(key, part):
    return block_table(key)


def draw_trip_in(key, part):
    return trip_slots(key, 31)


def draw_trip_out(key, part):
    return trip_slots(key, 32)


def touch_ends(drawn, rng, least, top_value):
    index_at = [jax.random.randint(jax.random.fold_in(rng, axis), (), 0, length) for axis, length in enumerate(drawn.shape)]
    main_axis = drawn.shape.index(max(drawn.shape))
    next_to = index_at[:main_axis] + [(index_at[main_axis] + 1) % drawn.shape[main_axis]] + index_at[main_axis + 1:]
    return drawn.at[tuple(index_at)].set(least).at[tuple(next_to)].set(top_value)


def level_of(rng, dims, pieces, low, top_value):
    factor_of, own = 1.0, jax.random.fold_in(rng, 6)
    for dim, shards_of in pieces:
        heights = jnp.exp(jax.random.uniform(jax.random.fold_in(own, dim), (shards_of,), jnp.float32, low / len(pieces), top_value / len(pieces)))
        factor_of = factor_of * jnp.repeat(heights, dims[dim] // shards_of).reshape([-1 if axis == dim else 1 for axis in range(len(dims))])
    return factor_of


def gaussian(rng, extent, width, most, split=(), kind=jnp.bfloat16):
    result = jax.random.normal(rng, extent, jnp.float32) * width
    if len(split) > 0:
        result = level_of(rng, extent, split, -0.22, 0.18) * result
    return jnp.clip(result, min=-most, max=most).astype(kind)


def setup_inputs(seed: int = 0, part: int = 0) -> dict:
    streams_of = jax.random.split(jax.random.key(seed), 15)
    own_keys = jax.random.split(jax.random.fold_in(streams_of[14], part), 15)
    return {
        "atom_state": gaussian(own_keys[0], (MB, ATOMS, D), 1.0, 6.0, ((0, 2), (1, 4))),
        "direction": gaussian(own_keys[1], (MB, ATOMS, D), 1.0, 6.0, ((0, 2), (1, 4))),
        "upstream": gaussian(own_keys[2], (MB, ATOMS, D), 1.0, 6.0, ((0, 2), (1, 4))),
        "edge_state": gaussian(own_keys[3], (MB, EDGES, D), 1.0, 6.0, ((0, 2), (1, 4))),
        "edge_src": touch_ends(jax.random.randint(own_keys[4], (MB, EDGES), 0, ATOMS), jax.random.fold_in(own_keys[4], 1), 0, ATOMS - 1).astype(jnp.int32),
        "edge_tgt": touch_ends(jax.random.randint(own_keys[5], (MB, EDGES), 0, ATOMS), jax.random.fold_in(own_keys[5], 1), 0, ATOMS - 1).astype(jnp.int32),
        "edge_blocks": draw_edge_blocks(jax.random.fold_in(jax.random.fold_in(streams_of[14], part), 71), part),
        "trip_in": draw_trip_in(jax.random.fold_in(jax.random.fold_in(streams_of[14], part), 71), part),
        "trip_out": draw_trip_out(jax.random.fold_in(jax.random.fold_in(streams_of[14], part), 71), part),
        "trip_coef": jnp.clip(jax.random.uniform(own_keys[9], (MB, TRIPS), jnp.float32, -1.0, 1.0) * level_of(own_keys[9], (MB, TRIPS), ((0, 2), (1, 4)), -0.4, 0.0), -1.0, 1.0).astype(jnp.bfloat16),
        "w_src": gaussian(streams_of[10], (D, D), D ** -0.5, 0.25),
        "w_tgt": gaussian(streams_of[11], (D, D), D ** -0.5, 0.25),
        "w_in": gaussian(streams_of[12], (D, HID), D ** -0.5, 0.25, ((1, 2),)),
        "w_out": gaussian(streams_of[13], (HID, D), (32 * HID) ** -0.5, 0.03125, ((0, 2),)),
    }


def project_high(values, weight):
    return jnp.dot(values, weight.astype(jnp.float32).T, precision=lax.Precision.HIGHEST, preferred_element_type=jnp.float32)


def micro_batch(atom_state, direction, upstream, edge_state, edge_src, edge_tgt, edge_blocks, trip_in, trip_out, trip_coef, w_src, w_tgt, w_in, w_out):
    slot_iota = jnp.arange(EDGES, dtype=jnp.int32)
    slot_owner = slot_iota // EDGE_DEV
    slot_mask = ((slot_iota % EDGE_DEV) < EBLOCK * edge_blocks[slot_owner]).astype(jnp.float32)[:, None]
    proj_src = jnp.dot(atom_state, w_src, preferred_element_type=jnp.float32).astype(jnp.bfloat16)
    proj_tgt = jnp.dot(atom_state, w_tgt, preferred_element_type=jnp.float32).astype(jnp.bfloat16)
    tan_src = jnp.dot(direction, w_src, preferred_element_type=jnp.float32).astype(jnp.bfloat16)
    tan_tgt = jnp.dot(direction, w_tgt, preferred_element_type=jnp.float32).astype(jnp.bfloat16)
    pre_edge = edge_state.astype(jnp.float32) + proj_src[edge_src].astype(jnp.float32) + proj_tgt[edge_tgt].astype(jnp.float32)
    tan_edge = tan_src[edge_src].astype(jnp.float32) + tan_tgt[edge_tgt].astype(jnp.float32)
    pre_low = pre_edge.astype(jnp.bfloat16)
    tan_low = tan_edge.astype(jnp.bfloat16)
    trip_base = (jnp.arange(TRIPS, dtype=jnp.int32) // TRIP_DEV) * EDGE_DEV
    in_edge = trip_base + trip_in
    out_edge = trip_base + trip_out
    coef_col = trip_coef.astype(jnp.float32)[:, None]
    mixed_sum = pre_edge + jax.ops.segment_sum(coef_col * pre_low[in_edge].astype(jnp.float32), out_edge, num_segments=EDGES)
    tan_mixed = tan_edge + jax.ops.segment_sum(coef_col * tan_low[in_edge].astype(jnp.float32), out_edge, num_segments=EDGES)
    mixed_low = mixed_sum.astype(jnp.bfloat16)
    tan_mixed_low = tan_mixed.astype(jnp.bfloat16)
    hidden_pre = jnp.dot(mixed_low, w_in, preferred_element_type=jnp.float32)
    tan_hidden = jnp.dot(tan_mixed_low, w_in, preferred_element_type=jnp.float32)
    sig_hidden = jax.nn.sigmoid(hidden_pre)
    activation = (hidden_pre * sig_hidden).astype(jnp.bfloat16)
    message = slot_mask * jnp.dot(activation, w_out, preferred_element_type=jnp.float32)
    atom_update = jax.ops.segment_sum(message, edge_tgt, num_segments=ATOMS).astype(jnp.bfloat16)
    edge_cot = (slot_mask * upstream[edge_tgt].astype(jnp.float32)).astype(jnp.bfloat16)
    act_cot = jnp.dot(edge_cot, w_out.T, preferred_element_type=jnp.float32)
    first_slope = sig_hidden * (1.0 + hidden_pre * (1.0 - sig_hidden))
    second_slope = sig_hidden * (1.0 - sig_hidden) * (2.0 + hidden_pre * (1.0 - 2.0 * sig_hidden))
    hid_cot = (act_cot * first_slope).astype(jnp.bfloat16)
    tan_hid_cot = (act_cot * second_slope * tan_hidden).astype(jnp.bfloat16)
    mix_cot = jnp.dot(hid_cot, w_in.T, preferred_element_type=jnp.float32)
    tan_mix_cot = jnp.dot(tan_hid_cot, w_in.T, preferred_element_type=jnp.float32)
    mix_cot_low = mix_cot.astype(jnp.bfloat16)
    tan_mix_cot_low = tan_mix_cot.astype(jnp.bfloat16)
    pre_cot = mix_cot + jax.ops.segment_sum(coef_col * mix_cot_low[out_edge].astype(jnp.float32), in_edge, num_segments=EDGES)
    tan_pre_cot = tan_mix_cot + jax.ops.segment_sum(coef_col * tan_mix_cot_low[out_edge].astype(jnp.float32), in_edge, num_segments=EDGES)
    pre_cot_low = pre_cot.astype(jnp.bfloat16).astype(jnp.float32)
    tan_pre_cot_low = tan_pre_cot.astype(jnp.bfloat16).astype(jnp.float32)
    grad_state = project_high(jax.ops.segment_sum(pre_cot_low, edge_src, num_segments=ATOMS), w_src) + project_high(jax.ops.segment_sum(pre_cot_low, edge_tgt, num_segments=ATOMS), w_tgt)
    hvp_state = project_high(jax.ops.segment_sum(tan_pre_cot_low, edge_src, num_segments=ATOMS), w_src) + project_high(jax.ops.segment_sum(tan_pre_cot_low, edge_tgt, num_segments=ATOMS), w_tgt)
    return atom_update, grad_state, hvp_state


def reference(atom_state, direction, upstream, edge_state, edge_src, edge_tgt, edge_blocks, trip_in, trip_out, trip_coef, w_src, w_tgt, w_in, w_out):
    results = [micro_batch(atom_state[batch_index], direction[batch_index], upstream[batch_index], edge_state[batch_index], edge_src[batch_index], edge_tgt[batch_index], edge_blocks[batch_index], trip_in[batch_index], trip_out[batch_index], trip_coef[batch_index], w_src, w_tgt, w_in, w_out) for batch_index in range(MB)]
    return (jnp.stack([result_item[0] for result_item in results]), jnp.stack([result_item[1] for result_item in results]), jnp.stack([result_item[2] for result_item in results]))
```

```python
import functools

import jax
import jax.numpy as jnp
from jax import lax
from jax.experimental import pallas as pl
from jax.experimental.pallas import tpu as pltpu
from jax.sharding import PartitionSpec as P

EBLOCK = 128
F32 = jnp.float32
BF16 = jnp.bfloat16
MESH = pl.DeviceIdType.MESH


def mm(a, b):
    return jnp.dot(a, b, preferred_element_type=F32)


def mm_nt(a, b):
    return lax.dot_general(a, b, (((1,), (1,)), ((), ())), preferred_element_type=F32)


def as_column(row):
    return jnp.transpose(jnp.broadcast_to(row, (8, row.shape[1])))[:, :1]


def split_rows(x):
    high = x.astype(BF16)
    return jnp.concatenate([high, (x - high.astype(F32)).astype(BF16)], axis=0)


def join_rows(x):
    half = x.shape[0] // 2
    return x[:half] + x[half:]


def kernel(
    n,
    state_ref,
    dir_ref,
    up_ref,
    src_ref,
    tgt_ref,
    blocks_ref,
    tin_ref,
    tout_ref,
    coef_ref,
    edge_hbm,
    wsrc_hbm,
    wtgt_hbm,
    win_hbm,
    wout_hbm,
    upd_out,
    grad_out,
    hvp_out,
    edge_v,
    wsrc_v,
    wtgt_v,
    win_v,
    wout_v,
    stage,
    gathered,
    upd_own,
    upd_send,
    upd_recv,
    cot_own,
    cot_send,
    cot_recv,
    pair_send,
    pair_recv,
    load_sem,
    g_send,
    g_recv,
    u_send,
    u_recv,
    c_send,
    c_recv,
    p_send,
    p_recv,
):
    me = lax.axis_index("graph")
    other = 1 - lax.axis_index("feat")
    atoms = state_ref.shape[1]
    width = state_ref.shape[2]
    all_atoms = n * atoms
    slots = src_ref.shape[1]
    trips = tin_ref.shape[1]
    half = width // 2

    loads = []
    for i, (s, d) in enumerate(
        (
            (edge_hbm.at[0], edge_v),
            (win_hbm, win_v),
            (wout_hbm, wout_v),
            (wsrc_hbm, wsrc_v),
            (wtgt_hbm, wtgt_v),
        )
    ):
        c = pltpu.make_async_copy(s, d, load_sem.at[i])
        c.start()
        loads.append(c)

    barrier = pltpu.get_barrier_semaphore()
    for k in range(1, n):
        pl.semaphore_signal(
            barrier, inc=1, device_id={"graph": lax.rem(me + k, n)}, device_id_type=MESH
        )
    pl.semaphore_signal(barrier, inc=1, device_id={"feat": other}, device_id_type=MESH)

    up = up_ref[0].astype(F32)
    mine = jnp.concatenate(
        [
            jnp.concatenate([state_ref[0].astype(F32), up[:, :half]], axis=1),
            jnp.concatenate([dir_ref[0].astype(F32), up[:, half:]], axis=1),
        ],
        axis=0,
    ).astype(BF16)
    stage[...] = mine
    gathered[me] = mine
    pl.semaphore_wait(barrier, n)

    gathers = []
    for k in range(1, n):
        c = pltpu.make_async_remote_copy(
            src_ref=stage,
            dst_ref=gathered.at[me],
            send_sem=g_send.at[k - 1],
            recv_sem=g_recv.at[k - 1],
            device_id={"graph": lax.rem(me + k, n)},
            device_id_type=MESH,
        )
        c.start()
        gathers.append(c)

    src_col = as_column(src_ref[...])
    tgt_row = tgt_ref[...]
    tgt_col = as_column(tgt_row)
    used = blocks_ref[0, 0] * EBLOCK
    pair = 2 * all_atoms
    lane = lax.broadcasted_iota(jnp.int32, (slots, 3 * pair), 1)
    base = jnp.where(lane >= 2 * pair, lane - 2 * pair, jnp.where(lane >= pair, lane - pair, lane))
    hot = ((base == src_col) | (base == tgt_col + all_atoms)).astype(F32)
    lane2 = lax.broadcasted_iota(jnp.int32, (slots, pair), 1)
    row2 = lax.broadcasted_iota(jnp.int32, (slots, pair), 0)
    tgt_hot = (
        ((lane2 == tgt_col) | (lane2 == tgt_col + all_atoms)) & (row2 < used)
    ).astype(F32).astype(BF16)
    atom_iota = lax.broadcasted_iota(jnp.int32, (all_atoms, slots), 0)
    slot_iota = lax.broadcasted_iota(jnp.int32, (all_atoms, slots), 1)
    tgt_hot_t = ((atom_iota == tgt_row) & (slot_iota < used)).astype(F32).astype(BF16)
    in_hot = (
        (lax.broadcasted_iota(jnp.int32, (trips, slots), 1) == as_column(tin_ref[...]))
        .astype(F32)
        .astype(BF16)
    )
    out_weighted = jnp.where(
        lax.broadcasted_iota(jnp.int32, (slots, trips), 0) == tout_ref[...],
        coef_ref[...].astype(F32),
        0.0,
    ).astype(BF16)
    hops = mm(in_hot, hot.astype(BF16)).astype(BF16)
    spread = hot + mm(out_weighted, hops)
    spread_high = spread.astype(BF16).astype(F32)
    spread_low = spread - spread_high
    spread_split = jnp.where((lane >= pair) & (lane < 2 * pair), spread_low, spread_high)
    spread_t = jnp.transpose(spread_split[:, : 2 * pair]).astype(BF16)
    spread_split = spread_split.astype(BF16)

    loads[0].wait()
    picked = mm(in_hot, edge_v[...]).astype(BF16)
    mixed = edge_v[...].astype(F32) + mm(out_weighted, picked)
    loads[1].wait()
    hidden_edge = mm(mixed.astype(BF16), win_v[...])
    for c in loads[2:]:
        c.wait()

    for c in gathers:
        c.wait_recv()
    rows = gathered[...].astype(F32)
    state = rows[:, :atoms, :width].reshape(all_atoms, width)
    direction = rows[:, atoms:, :width].reshape(all_atoms, width)
    upstream = jnp.concatenate(
        [
            rows[:, :atoms, width:].reshape(all_atoms, half),
            rows[:, atoms:, width:].reshape(all_atoms, half),
        ],
        axis=1,
    ).astype(BF16)
    both = jnp.concatenate([state, direction], axis=0).astype(BF16)
    proj_src = mm(both, wsrc_v[...])
    proj_tgt = mm(both, wtgt_v[...])
    proj = jnp.concatenate(
        [
            proj_src[:all_atoms],
            proj_tgt[:all_atoms],
            proj_src[all_atoms:],
            proj_tgt[all_atoms:],
        ],
        axis=0,
    ).astype(BF16)
    proj_hidden = mm(proj, win_v[...])
    high = proj_hidden.astype(BF16)
    low = (proj_hidden - high.astype(F32)).astype(BF16)
    hidden_pre = hidden_edge + mm(
        spread_split, jnp.concatenate([high[:pair], high[:pair], low[:pair]], axis=0)
    )
    tan_hidden = mm(
        spread_split, jnp.concatenate([high[pair:], high[pair:], low[pair:]], axis=0)
    )
    act_cot = mm(tgt_hot, split_rows(mm_nt(upstream, wout_v[...])))

    sig = jax.nn.sigmoid(hidden_pre)
    activation = (hidden_pre * sig).astype(BF16)
    rest = 1.0 - sig
    first_slope = sig * (1.0 + hidden_pre * rest)
    second_slope = sig * rest * (2.0 + hidden_pre * (1.0 - 2.0 * sig))
    hid_cot = (act_cot * first_slope).astype(BF16)
    tan_hid_cot = (act_cot * second_slope * tan_hidden).astype(BF16)

    update = join_rows(mm(split_rows(mm(tgt_hot_t, activation)), wout_v[...]))
    for p in range(n):
        part = update[p * atoms : (p + 1) * atoms]
        packed = jnp.concatenate([part[:, :half], part[:, half:]], axis=0)
        upd_own[p] = packed
        upd_send[p] = packed.astype(BF16)
    updates = []
    for k in range(1, n):
        peer = lax.rem(me + k, n)
        c = pltpu.make_async_remote_copy(
            src_ref=upd_send.at[peer],
            dst_ref=upd_recv.at[k - 1],
            send_sem=u_send.at[k - 1],
            recv_sem=u_recv.at[k - 1],
            device_id={"graph": peer},
            device_id_type=MESH,
        )
        c.start()
        updates.append(c)

    via = jnp.concatenate(
        [join_rows(mm(spread_t, hid_cot)), join_rows(mm(spread_t, tan_hid_cot))], axis=0
    )
    via = join_rows(mm_nt(split_rows(via), win_v[...]))
    via_src = jnp.concatenate([via[:all_atoms], via[pair : pair + all_atoms]], axis=0)
    via_tgt = jnp.concatenate([via[all_atoms:pair], via[pair + all_atoms :]], axis=0)
    grads = join_rows(
        mm_nt(split_rows(via_src), wsrc_v[...]) + mm_nt(split_rows(via_tgt), wtgt_v[...])
    )
    for p in range(n):
        packed = jnp.concatenate(
            [
                grads[p * atoms : (p + 1) * atoms],
                grads[all_atoms + p * atoms : all_atoms + (p + 1) * atoms],
            ],
            axis=0,
        )
        cot_own[p] = packed
        cot_send[p] = packed.astype(BF16)
    cots = []
    for k in range(1, n):
        peer = lax.rem(me + k, n)
        c = pltpu.make_async_remote_copy(
            src_ref=cot_send.at[peer],
            dst_ref=cot_recv.at[k - 1],
            send_sem=c_send.at[k - 1],
            recv_sem=c_recv.at[k - 1],
            device_id={"graph": peer},
            device_id_type=MESH,
        )
        c.start()
        cots.append(c)

    upd_sum = upd_own[me]
    for k in range(1, n):
        updates[k - 1].wait_recv()
        upd_sum = upd_sum + upd_recv[k - 1].astype(F32)
    cot_sum = cot_own[me]
    for k in range(1, n):
        cots[k - 1].wait_recv()
        cot_sum = cot_sum + cot_recv[k - 1].astype(F32)
    total = jnp.concatenate([cot_sum, upd_sum], axis=1)
    pair_send[...] = total
    c = pltpu.make_async_remote_copy(
        src_ref=pair_send,
        dst_ref=pair_recv,
        send_sem=p_send,
        recv_sem=p_recv,
        device_id={"feat": other},
        device_id_type=MESH,
    )
    c.start()
    c.wait_recv()
    total = total + pair_recv[...]
    grad_out[0] = total[:atoms, :width]
    hvp_out[0] = total[atoms:, :width]
    upd_out[0] = jnp.concatenate([total[:atoms, width:], total[atoms:, width:]], axis=1).astype(
        BF16
    )
    c.wait_send()
    for c in gathers + updates + cots:
        c.wait_send()


def on_device(
    atom_state,
    direction,
    upstream,
    edge_state,
    edge_src,
    edge_tgt,
    edge_blocks,
    trip_in,
    trip_out,
    trip_coef,
    w_src,
    w_tgt,
    w_in,
    w_out,
):
    n = lax.axis_size("graph")
    atoms, width = atom_state.shape[1:]
    slots = edge_state.shape[1]
    hidden = w_in.shape[1]
    half = width // 2
    vmem = pl.BlockSpec(memory_space=pltpu.VMEM)
    smem = pl.BlockSpec(memory_space=pltpu.SMEM)
    far = pl.BlockSpec(memory_space=pl.ANY)
    dma = pltpu.SemaphoreType.DMA
    return pl.pallas_call(
        functools.partial(kernel, n),
        name="interaction",
        out_shape=(
            jax.ShapeDtypeStruct((1, atoms, width), BF16),
            jax.ShapeDtypeStruct((1, atoms, width), F32),
            jax.ShapeDtypeStruct((1, atoms, width), F32),
        ),
        in_specs=[vmem] * 5 + [smem] + [vmem] * 3 + [far] * 5,
        out_specs=(vmem, vmem, vmem),
        scratch_shapes=[
            pltpu.VMEM((slots, width), BF16),
            pltpu.VMEM((width, width), BF16),
            pltpu.VMEM((width, width), BF16),
            pltpu.VMEM((width, hidden), BF16),
            pltpu.VMEM((hidden, width), BF16),
            pltpu.VMEM((2 * atoms, width + half), BF16),
            pltpu.VMEM((n, 2 * atoms, width + half), BF16),
            pltpu.VMEM((n, 2 * atoms, half), F32),
            pltpu.VMEM((n, 2 * atoms, half), BF16),
            pltpu.VMEM((n - 1, 2 * atoms, half), BF16),
            pltpu.VMEM((n, 2 * atoms, width), F32),
            pltpu.VMEM((n, 2 * atoms, width), BF16),
            pltpu.VMEM((n - 1, 2 * atoms, width), BF16),
            pltpu.VMEM((2 * atoms, width + half), F32),
            pltpu.VMEM((2 * atoms, width + half), F32),
            dma((5,)),
            dma((n - 1,)),
            dma((n - 1,)),
            dma((n - 1,)),
            dma((n - 1,)),
            dma((n - 1,)),
            dma((n - 1,)),
            dma,
            dma,
        ],
        compiler_params=pltpu.CompilerParams(
            collective_id=0, has_side_effects=True, vmem_limit_bytes=48 * 1024 * 1024
        ),
    )(
        atom_state,
        direction,
        upstream,
        edge_src,
        edge_tgt,
        edge_blocks,
        trip_in,
        trip_out,
        trip_coef,
        edge_state,
        w_src,
        w_tgt,
        w_in,
        w_out,
    )


def solution(mesh):
    in_specs = (
        P(("groups", "pipe"), "graph", None),
        P(("groups", "pipe"), "graph", None),
        P(("groups", "pipe"), "graph", None),
        P(("groups", "pipe"), "graph", None),
        P(("groups", "pipe"), "graph"),
        P(("groups", "pipe"), "graph"),
        P(("groups", "pipe"), "graph"),
        P(("groups", "pipe"), "graph"),
        P(("groups", "pipe"), "graph"),
        P(("groups", "pipe"), "graph"),
        P(),
        P(),
        P(None, "feat"),
        P("feat", None),
    )
    out_specs = (
        P(("groups", "pipe"), "graph", None),
        P(("groups", "pipe"), "graph", None),
        P(("groups", "pipe"), "graph", None),
    )
    return jax.shard_map(
        on_device, mesh=mesh, in_specs=in_specs, out_specs=out_specs, check_vma=False
    )
```

```python
import functools

import jax
import jax.numpy as jnp
from jax import lax
from jax.experimental import pallas as pl
from jax.experimental.pallas import tpu as pltpu
from jax.sharding import PartitionSpec as P

EBLOCK = 128
F32 = jnp.float32
BF16 = jnp.bfloat16
MESH = pl.DeviceIdType.MESH


def mm(a, b):
    return jnp.dot(a, b, preferred_element_type=F32)


def mm_nt(a, b):
    return lax.dot_general(a, b, (((1,), (1,)), ((), ())), preferred_element_type=F32)


def as_column(row):
    return jnp.transpose(jnp.broadcast_to(row, (8, row.shape[1])))[:, :1]


def split_rows(x):
    high = x.astype(BF16)
    return jnp.concatenate([high, (x - high.astype(F32)).astype(BF16)], axis=0)


def join_rows(x):
    half = x.shape[0] // 2
    return x[:half] + x[half:]


def peers_of(me, n):
    if n & (n - 1):
        return [lax.rem(me + k, n) for k in range(1, n)]
    peers = []
    for j in range(n - 1, 0, -1):
        peer, bit = me, 1
        while bit < n:
            if j & bit:
                peer = peer + bit * (1 - 2 * lax.rem(me // bit, 2))
            bit *= 2
        peers.append(peer)
    return peers


def kernel(
    n,
    state_hbm,
    dir_hbm,
    up_hbm,
    src_hbm,
    tgt_hbm,
    blocks_hbm,
    tin_hbm,
    tout_hbm,
    coef_hbm,
    edge_hbm,
    wsrc_hbm,
    wtgt_hbm,
    win_hbm,
    wout_hbm,
    upd_hbm,
    grad_hbm,
    hvp_hbm,
    state_ref,
    dir_ref,
    up_ref,
    src_ref,
    tgt_ref,
    blocks_ref,
    tin_ref,
    tout_ref,
    coef_ref,
    edge_v,
    wsrc_v,
    wtgt_v,
    win_v,
    wout_v,
    stage,
    gathered,
    upd_own,
    upd_send,
    upd_recv,
    cot_own,
    cot_send,
    cot_recv,
    pair_send,
    pair_recv,
    load_sem,
    g_send,
    g_recv,
    u_send,
    u_recv,
    c_send,
    c_recv,
    p_send,
    p_recv,
    upd_v,
    grad_v,
    hvp_v,
    store_sem,
):
    me = lax.axis_index("graph")
    other = 1 - lax.axis_index("feat")
    atoms = state_ref.shape[1]
    width = state_ref.shape[2]
    all_atoms = n * atoms
    slots = src_ref.shape[1]
    trips = tin_ref.shape[1]
    half = width // 2

    peers = peers_of(me, n)
    barrier = pltpu.get_barrier_semaphore()
    for peer in peers:
        pl.semaphore_signal(barrier, inc=1, device_id={"graph": peer}, device_id_type=MESH)
    pl.semaphore_signal(barrier, inc=1, device_id={"feat": other}, device_id_type=MESH)

    loads = []
    for i, (s, d) in enumerate(
        (
            (state_hbm, state_ref),
            (dir_hbm, dir_ref),
            (up_hbm, up_ref),
            (src_hbm, src_ref),
            (tgt_hbm, tgt_ref),
            (tin_hbm, tin_ref),
            (tout_hbm, tout_ref),
            (coef_hbm, coef_ref),
            (blocks_hbm, blocks_ref),
            (edge_hbm.at[0], edge_v),
            (win_hbm, win_v),
            (wout_hbm, wout_v),
            (wsrc_hbm, wsrc_v),
            (wtgt_hbm, wtgt_v),
        )
    ):
        c = pltpu.make_async_copy(s, d, load_sem.at[i])
        c.start()
        loads.append(c)

    for c in loads[:3]:
        c.wait()
    up = up_ref[0].astype(F32)
    mine = jnp.concatenate(
        [
            jnp.concatenate([state_ref[0].astype(F32), up[:, :half]], axis=1),
            jnp.concatenate([dir_ref[0].astype(F32), up[:, half:]], axis=1),
        ],
        axis=0,
    ).astype(BF16)
    stage[...] = mine
    gathered[me] = mine
    pl.semaphore_wait(barrier, n)

    gathers = []
    for k, peer in enumerate(peers):
        c = pltpu.make_async_remote_copy(
            src_ref=stage,
            dst_ref=gathered.at[me],
            send_sem=g_send.at[k],
            recv_sem=g_recv.at[k],
            device_id={"graph": peer},
            device_id_type=MESH,
        )
        c.start()
        gathers.append(c)

    for c in loads[3:9]:
        c.wait()
    src_col = as_column(src_ref[...])
    tgt_row = tgt_ref[...]
    tgt_col = as_column(tgt_row)
    used = blocks_ref[0, 0] * EBLOCK
    pair = 2 * all_atoms
    lane = lax.broadcasted_iota(jnp.int32, (slots, 3 * pair), 1)
    base = jnp.where(lane >= 2 * pair, lane - 2 * pair, jnp.where(lane >= pair, lane - pair, lane))
    hot = ((base == src_col) | (base == tgt_col + all_atoms)).astype(F32)
    lane2 = lax.broadcasted_iota(jnp.int32, (slots, pair), 1)
    row2 = lax.broadcasted_iota(jnp.int32, (slots, pair), 0)
    tgt_hot = (
        ((lane2 == tgt_col) | (lane2 == tgt_col + all_atoms)) & (row2 < used)
    ).astype(F32).astype(BF16)
    atom_iota = lax.broadcasted_iota(jnp.int32, (all_atoms, slots), 0)
    slot_iota = lax.broadcasted_iota(jnp.int32, (all_atoms, slots), 1)
    tgt_hot_t = ((atom_iota == tgt_row) & (slot_iota < used)).astype(F32).astype(BF16)
    in_hot = (
        (lax.broadcasted_iota(jnp.int32, (trips, slots), 1) == as_column(tin_ref[...]))
        .astype(F32)
        .astype(BF16)
    )
    out_weighted = jnp.where(
        lax.broadcasted_iota(jnp.int32, (slots, trips), 0) == tout_ref[...],
        coef_ref[...].astype(F32),
        0.0,
    ).astype(BF16)
    hops = mm(in_hot, hot.astype(BF16)).astype(BF16)
    spread = hot + mm(out_weighted, hops)
    spread_high = spread.astype(BF16).astype(F32)
    spread_low = spread - spread_high
    spread_split = jnp.where((lane >= pair) & (lane < 2 * pair), spread_low, spread_high)
    spread_t = jnp.transpose(spread_split[:, : 2 * pair]).astype(BF16)
    spread_split = spread_split.astype(BF16)

    loads[9].wait()
    picked = mm(in_hot, edge_v[...]).astype(BF16)
    mixed = edge_v[...].astype(F32) + mm(out_weighted, picked)
    loads[10].wait()
    hidden_edge = mm(mixed.astype(BF16), win_v[...])
    for c in loads[11:]:
        c.wait()
    src_in = mm(wsrc_v[...], win_v[...]).astype(BF16)
    tgt_in = mm(wtgt_v[...], win_v[...]).astype(BF16)

    for c in gathers:
        c.wait_recv()
    rows = gathered[...].astype(F32)
    state = rows[:, :atoms, :width].reshape(all_atoms, width)
    direction = rows[:, atoms:, :width].reshape(all_atoms, width)
    upstream = jnp.concatenate(
        [
            rows[:, :atoms, width:].reshape(all_atoms, half),
            rows[:, atoms:, width:].reshape(all_atoms, half),
        ],
        axis=1,
    ).astype(BF16)
    both = jnp.concatenate([state, direction], axis=0).astype(BF16)
    via_src = mm(both, src_in)
    via_tgt = mm(both, tgt_in)
    proj_hidden = jnp.concatenate(
        [via_src[:all_atoms], via_tgt[:all_atoms], via_src[all_atoms:], via_tgt[all_atoms:]],
        axis=0,
    )
    high = proj_hidden.astype(BF16)
    low = (proj_hidden - high.astype(F32)).astype(BF16)
    hidden_pre = hidden_edge + mm(
        spread_split, jnp.concatenate([high[:pair], high[:pair], low[:pair]], axis=0)
    )
    tan_hidden = mm(
        spread_split, jnp.concatenate([high[pair:], high[pair:], low[pair:]], axis=0)
    )
    act_cot = mm(tgt_hot, split_rows(mm_nt(upstream, wout_v[...])))

    sig = jax.nn.sigmoid(hidden_pre)
    activation = (hidden_pre * sig).astype(BF16)
    rest = 1.0 - sig
    first_slope = sig * (1.0 + hidden_pre * rest)
    second_slope = sig * rest * (2.0 + hidden_pre * (1.0 - 2.0 * sig))
    hid_cot = (act_cot * first_slope).astype(BF16)
    tan_hid_cot = (act_cot * second_slope * tan_hidden).astype(BF16)

    update = join_rows(mm(split_rows(mm(tgt_hot_t, activation)), wout_v[...]))
    for p in range(n):
        part = update[p * atoms : (p + 1) * atoms]
        packed = jnp.concatenate([part[:, :half], part[:, half:]], axis=0)
        upd_own[p] = packed
        upd_send[p] = packed.astype(BF16)
    updates = []
    for k, peer in enumerate(peers):
        c = pltpu.make_async_remote_copy(
            src_ref=upd_send.at[peer],
            dst_ref=upd_recv.at[k],
            send_sem=u_send.at[k],
            recv_sem=u_recv.at[k],
            device_id={"graph": peer},
            device_id_type=MESH,
        )
        c.start()
        updates.append(c)

    via = jnp.concatenate(
        [join_rows(mm(spread_t, hid_cot)), join_rows(mm(spread_t, tan_hid_cot))], axis=0
    )
    via_src = jnp.concatenate([via[:all_atoms], via[pair : pair + all_atoms]], axis=0)
    via_tgt = jnp.concatenate([via[all_atoms:pair], via[pair + all_atoms :]], axis=0)
    grads = join_rows(mm_nt(split_rows(via_src), src_in) + mm_nt(split_rows(via_tgt), tgt_in))
    for p in range(n):
        packed = jnp.concatenate(
            [
                grads[p * atoms : (p + 1) * atoms],
                grads[all_atoms + p * atoms : all_atoms + (p + 1) * atoms],
            ],
            axis=0,
        )
        cot_own[p] = packed
        cot_send[p] = packed.astype(BF16)
    cots = []
    for k, peer in enumerate(peers):
        c = pltpu.make_async_remote_copy(
            src_ref=cot_send.at[peer],
            dst_ref=cot_recv.at[k],
            send_sem=c_send.at[k],
            recv_sem=c_recv.at[k],
            device_id={"graph": peer},
            device_id_type=MESH,
        )
        c.start()
        cots.append(c)

    upd_sum = upd_own[me]
    for k in range(n - 1):
        updates[k].wait_recv()
        upd_sum = upd_sum + upd_recv[k].astype(F32)
    cot_sum = cot_own[me]
    for k in range(n - 1):
        cots[k].wait_recv()
        cot_sum = cot_sum + cot_recv[k].astype(F32)
    total = jnp.concatenate([cot_sum, upd_sum], axis=1)
    pair_send[...] = total
    c = pltpu.make_async_remote_copy(
        src_ref=pair_send,
        dst_ref=pair_recv,
        send_sem=p_send,
        recv_sem=p_recv,
        device_id={"feat": other},
        device_id_type=MESH,
    )
    c.start()
    c.wait_recv()
    total = total + pair_recv[...]
    upd_v[0] = jnp.concatenate([total[:atoms, width:], total[atoms:, width:]], axis=1).astype(BF16)
    grad_v[0] = total[:atoms, :width]
    hvp_v[0] = total[atoms:, :width]
    stores = [
        pltpu.make_async_copy(v, hbm, store_sem.at[i])
        for i, (v, hbm) in enumerate(((upd_v, upd_hbm), (grad_v, grad_hbm), (hvp_v, hvp_hbm)))
    ]
    for s in stores:
        s.start()
    c.wait_send()
    for c in gathers + updates + cots:
        c.wait_send()
    for s in stores:
        s.wait()


def write_out(upd_ref, grad_ref, hvp_ref, upd_out, grad_out, hvp_out):
    upd_out[...] = upd_ref[...]
    grad_out[...] = grad_ref[...]
    hvp_out[...] = hvp_ref[...]


def on_device(
    atom_state,
    direction,
    upstream,
    edge_state,
    edge_src,
    edge_tgt,
    edge_blocks,
    trip_in,
    trip_out,
    trip_coef,
    w_src,
    w_tgt,
    w_in,
    w_out,
):
    n = lax.axis_size("graph")
    atoms, width = atom_state.shape[1:]
    slots = edge_state.shape[1]
    hidden = w_in.shape[1]
    half = width // 2
    trips = trip_in.shape[1]
    far = pl.BlockSpec(memory_space=pltpu.HBM)
    dma = pltpu.SemaphoreType.DMA
    outs = (
        jax.ShapeDtypeStruct((1, atoms, width), BF16),
        jax.ShapeDtypeStruct((1, atoms, width), F32),
        jax.ShapeDtypeStruct((1, atoms, width), F32),
    )
    results = pl.pallas_call(
        functools.partial(kernel, n),
        name="interaction",
        out_shape=outs,
        in_specs=[far] * 14,
        out_specs=(far, far, far),
        scratch_shapes=[
            pltpu.VMEM((1, atoms, width), BF16),
            pltpu.VMEM((1, atoms, width), BF16),
            pltpu.VMEM((1, atoms, width), BF16),
            pltpu.VMEM((1, slots), jnp.int32),
            pltpu.VMEM((1, slots), jnp.int32),
            pltpu.SMEM((1, 1), jnp.int32),
            pltpu.VMEM((1, trips), jnp.int32),
            pltpu.VMEM((1, trips), jnp.int32),
            pltpu.VMEM((1, trips), BF16),
            pltpu.VMEM((slots, width), BF16),
            pltpu.VMEM((width, width), BF16),
            pltpu.VMEM((width, width), BF16),
            pltpu.VMEM((width, hidden), BF16),
            pltpu.VMEM((hidden, width), BF16),
            pltpu.VMEM((2 * atoms, width + half), BF16),
            pltpu.VMEM((n, 2 * atoms, width + half), BF16),
            pltpu.VMEM((n, 2 * atoms, half), F32),
            pltpu.VMEM((n, 2 * atoms, half), BF16),
            pltpu.VMEM((n - 1, 2 * atoms, half), BF16),
            pltpu.VMEM((n, 2 * atoms, width), F32),
            pltpu.VMEM((n, 2 * atoms, width), BF16),
            pltpu.VMEM((n - 1, 2 * atoms, width), BF16),
            pltpu.VMEM((2 * atoms, width + half), F32),
            pltpu.VMEM((2 * atoms, width + half), F32),
            dma((14,)),
            dma((n - 1,)),
            dma((n - 1,)),
            dma((n - 1,)),
            dma((n - 1,)),
            dma((n - 1,)),
            dma((n - 1,)),
            dma,
            dma,
        ]
        + [pltpu.VMEM(o.shape, o.dtype) for o in outs]
        + [dma((3,))],
        compiler_params=pltpu.CompilerParams(
            collective_id=0, has_side_effects=True, vmem_limit_bytes=64 * 1024 * 1024
        ),
    )(
        atom_state,
        direction,
        upstream,
        edge_src,
        edge_tgt,
        edge_blocks,
        trip_in,
        trip_out,
        trip_coef,
        edge_state,
        w_src,
        w_tgt,
        w_in,
        w_out,
    )
    return pl.pallas_call(
        write_out,
        name="write_out",
        out_shape=outs,
        compiler_params=pltpu.CompilerParams(vmem_limit_bytes=64 * 1024 * 1024),
    )(*results)


def solution(mesh):
    in_specs = (
        P(("groups", "pipe"), "graph", None),
        P(("groups", "pipe"), "graph", None),
        P(("groups", "pipe"), "graph", None),
        P(("groups", "pipe"), "graph", None),
        P(("groups", "pipe"), "graph"),
        P(("groups", "pipe"), "graph"),
        P(("groups", "pipe"), "graph"),
        P(("groups", "pipe"), "graph"),
        P(("groups", "pipe"), "graph"),
        P(("groups", "pipe"), "graph"),
        P(),
        P(),
        P(None, "feat"),
        P("feat", None),
    )
    out_specs = (
        P(("groups", "pipe"), "graph", None),
        P(("groups", "pipe"), "graph", None),
        P(("groups", "pipe"), "graph", None),
    )
    return jax.shard_map(
        on_device, mesh=mesh, in_specs=in_specs, out_specs=out_specs, check_vma=False
    )
```

```python
import functools

import jax
import jax.numpy as jnp
from jax import lax
from jax.experimental import pallas as pl
from jax.experimental.pallas import tpu as pltpu
from jax.sharding import PartitionSpec as P

EBLOCK = 128
F32 = jnp.float32
BF16 = jnp.bfloat16
MESH = pl.DeviceIdType.MESH


def mm(a, b):
    return jnp.dot(a, b, preferred_element_type=F32)


def mm_nt(a, b):
    return lax.dot_general(a, b, (((1,), (1,)), ((), ())), preferred_element_type=F32)


def as_column(row):
    return jnp.transpose(jnp.broadcast_to(row, (8, row.shape[1])))[:, :1]


def split_rows(x):
    high = x.astype(BF16)
    return jnp.concatenate([high, (x - high.astype(F32)).astype(BF16)], axis=0)


def join_rows(x):
    half = x.shape[0] // 2
    return x[:half] + x[half:]


def peers_of(me, n):
    if n & (n - 1):
        return [lax.rem(me + k, n) for k in range(1, n)]
    peers = []
    for j in range(n - 1, 0, -1):
        peer, bit = me, 1
        while bit < n:
            if j & bit:
                peer = peer + bit * (1 - 2 * lax.rem(me // bit, 2))
            bit *= 2
        peers.append(peer)
    return peers


def kernel(
    n,
    state_hbm,
    dir_hbm,
    up_hbm,
    src_hbm,
    tgt_hbm,
    blocks_hbm,
    tin_hbm,
    tout_hbm,
    coef_hbm,
    edge_hbm,
    wsrc_hbm,
    wtgt_hbm,
    win_hbm,
    wout_hbm,
    upd_hbm,
    grad_hbm,
    hvp_hbm,
    state_ref,
    dir_ref,
    up_ref,
    src_ref,
    tgt_ref,
    blocks_ref,
    tin_ref,
    tout_ref,
    coef_ref,
    edge_v,
    wsrc_v,
    wtgt_v,
    win_v,
    wout_v,
    stage,
    gathered,
    upd_own,
    upd_send,
    upd_recv,
    cot_own,
    cot_send,
    cot_recv,
    pair_send,
    pair_recv,
    load_sem,
    g_send,
    g_recv,
    u_send,
    u_recv,
    c_send,
    c_recv,
    p_send,
    p_recv,
    upd_v,
    grad_v,
    hvp_v,
    store_sem,
):
    me = lax.axis_index("graph")
    other = 1 - lax.axis_index("feat")
    atoms = state_ref.shape[1]
    width = state_ref.shape[2]
    all_atoms = n * atoms
    slots = src_ref.shape[1]
    trips = tin_ref.shape[1]
    half = width // 2

    peers = peers_of(me, n)
    barrier = pltpu.get_barrier_semaphore()
    for peer in peers:
        pl.semaphore_signal(barrier, inc=1, device_id={"graph": peer}, device_id_type=MESH)
    pl.semaphore_signal(barrier, inc=1, device_id={"feat": other}, device_id_type=MESH)

    loads = []
    for i, (s, d) in enumerate(
        (
            (state_hbm, state_ref),
            (dir_hbm, dir_ref),
            (up_hbm, up_ref),
            (src_hbm, src_ref),
            (tgt_hbm, tgt_ref),
            (tin_hbm, tin_ref),
            (tout_hbm, tout_ref),
            (coef_hbm, coef_ref),
            (blocks_hbm, blocks_ref),
            (edge_hbm.at[0], edge_v),
            (win_hbm, win_v),
            (wout_hbm, wout_v),
            (wsrc_hbm, wsrc_v),
            (wtgt_hbm, wtgt_v),
        )
    ):
        c = pltpu.make_async_copy(s, d, load_sem.at[i])
        c.start()
        loads.append(c)

    for c in loads[:3]:
        c.wait()
    up = up_ref[0].astype(F32)
    mine = jnp.concatenate(
        [
            jnp.concatenate([state_ref[0].astype(F32), up[:, :half]], axis=1),
            jnp.concatenate([dir_ref[0].astype(F32), up[:, half:]], axis=1),
        ],
        axis=0,
    ).astype(BF16)
    stage[...] = mine
    gathered[me] = mine
    for c in loads[3:9]:
        c.wait()
    src_col = as_column(src_ref[...])
    tgt_row = tgt_ref[...]
    tgt_col = as_column(tgt_row)
    used = blocks_ref[0, 0] * EBLOCK
    pair = 2 * all_atoms
    lane = lax.broadcasted_iota(jnp.int32, (slots, 3 * pair), 1)
    base = jnp.where(lane >= 2 * pair, lane - 2 * pair, jnp.where(lane >= pair, lane - pair, lane))
    hot = ((base == src_col) | (base == tgt_col + all_atoms)).astype(F32)
    lane2 = lax.broadcasted_iota(jnp.int32, (slots, pair), 1)
    row2 = lax.broadcasted_iota(jnp.int32, (slots, pair), 0)
    tgt_hot = (
        ((lane2 == tgt_col) | (lane2 == tgt_col + all_atoms)) & (row2 < used)
    ).astype(F32).astype(BF16)
    atom_iota = lax.broadcasted_iota(jnp.int32, (all_atoms, slots), 0)
    slot_iota = lax.broadcasted_iota(jnp.int32, (all_atoms, slots), 1)
    tgt_hot_t = ((atom_iota == tgt_row) & (slot_iota < used)).astype(F32).astype(BF16)
    in_hot = (
        (lax.broadcasted_iota(jnp.int32, (trips, slots), 1) == as_column(tin_ref[...]))
        .astype(F32)
        .astype(BF16)
    )
    out_weighted = jnp.where(
        lax.broadcasted_iota(jnp.int32, (slots, trips), 0) == tout_ref[...],
        coef_ref[...].astype(F32),
        0.0,
    ).astype(BF16)
    hops = mm(in_hot, hot.astype(BF16)).astype(BF16)
    spread = hot + mm(out_weighted, hops)
    spread_high = spread.astype(BF16).astype(F32)
    spread_low = spread - spread_high
    spread_split = jnp.where((lane >= pair) & (lane < 2 * pair), spread_low, spread_high)
    spread_t = jnp.transpose(spread_split[:, : 2 * pair]).astype(BF16)
    spread_split = spread_split.astype(BF16)

    pl.semaphore_wait(barrier, n)

    gathers = []
    for k, peer in enumerate(peers):
        c = pltpu.make_async_remote_copy(
            src_ref=stage,
            dst_ref=gathered.at[me],
            send_sem=g_send.at[k],
            recv_sem=g_recv.at[k],
            device_id={"graph": peer},
            device_id_type=MESH,
        )
        c.start()
        gathers.append(c)

    loads[9].wait()
    picked = mm(in_hot, edge_v[...]).astype(BF16)
    mixed = edge_v[...].astype(F32) + mm(out_weighted, picked)
    loads[10].wait()
    hidden_edge = mm(mixed.astype(BF16), win_v[...])
    for c in loads[11:]:
        c.wait()
    src_in = mm(wsrc_v[...], win_v[...]).astype(BF16)
    tgt_in = mm(wtgt_v[...], win_v[...]).astype(BF16)

    for c in gathers:
        c.wait_recv()
    rows = gathered[...].astype(F32)
    state = rows[:, :atoms, :width].reshape(all_atoms, width)
    direction = rows[:, atoms:, :width].reshape(all_atoms, width)
    upstream = jnp.concatenate(
        [
            rows[:, :atoms, width:].reshape(all_atoms, half),
            rows[:, atoms:, width:].reshape(all_atoms, half),
        ],
        axis=1,
    ).astype(BF16)
    both = jnp.concatenate([state, direction], axis=0).astype(BF16)
    via_src = mm(both, src_in)
    via_tgt = mm(both, tgt_in)
    proj_hidden = jnp.concatenate(
        [via_src[:all_atoms], via_tgt[:all_atoms], via_src[all_atoms:], via_tgt[all_atoms:]],
        axis=0,
    )
    high = proj_hidden.astype(BF16)
    low = (proj_hidden - high.astype(F32)).astype(BF16)
    hidden_pre = hidden_edge + mm(
        spread_split, jnp.concatenate([high[:pair], high[:pair], low[:pair]], axis=0)
    )
    tan_hidden = mm(
        spread_split, jnp.concatenate([high[pair:], high[pair:], low[pair:]], axis=0)
    )
    act_cot = mm(tgt_hot, split_rows(mm_nt(upstream, wout_v[...])))

    tanh = jnp.tanh(0.5 * hidden_pre)
    sig = 0.5 + 0.5 * tanh
    bell = 0.25 - 0.25 * (tanh * tanh)
    activation = (hidden_pre * sig).astype(BF16)
    first_slope = sig + hidden_pre * bell
    second_slope = bell * (2.0 - hidden_pre * tanh)
    hid_cot = (act_cot * first_slope).astype(BF16)
    tan_hid_cot = (act_cot * second_slope * tan_hidden).astype(BF16)

    update = join_rows(mm(split_rows(mm(tgt_hot_t, activation)), wout_v[...]))
    for p in range(n):
        part = update[p * atoms : (p + 1) * atoms]
        packed = jnp.concatenate([part[:, :half], part[:, half:]], axis=0)
        upd_own[p] = packed
        upd_send[p] = packed.astype(BF16)
    updates = []
    for k, peer in enumerate(peers):
        c = pltpu.make_async_remote_copy(
            src_ref=upd_send.at[peer],
            dst_ref=upd_recv.at[k],
            send_sem=u_send.at[k],
            recv_sem=u_recv.at[k],
            device_id={"graph": peer},
            device_id_type=MESH,
        )
        c.start()
        updates.append(c)

    via = jnp.concatenate(
        [join_rows(mm(spread_t, hid_cot)), join_rows(mm(spread_t, tan_hid_cot))], axis=0
    )
    via_src = jnp.concatenate([via[:all_atoms], via[pair : pair + all_atoms]], axis=0)
    via_tgt = jnp.concatenate([via[all_atoms:pair], via[pair + all_atoms :]], axis=0)
    grads = join_rows(mm_nt(split_rows(via_src), src_in) + mm_nt(split_rows(via_tgt), tgt_in))
    for p in range(n):
        packed = jnp.concatenate(
            [
                grads[p * atoms : (p + 1) * atoms],
                grads[all_atoms + p * atoms : all_atoms + (p + 1) * atoms],
            ],
            axis=0,
        )
        cot_own[p] = packed
        cot_send[p] = packed.astype(BF16)
    cots = []
    for k, peer in enumerate(peers):
        c = pltpu.make_async_remote_copy(
            src_ref=cot_send.at[peer],
            dst_ref=cot_recv.at[k],
            send_sem=c_send.at[k],
            recv_sem=c_recv.at[k],
            device_id={"graph": peer},
            device_id_type=MESH,
        )
        c.start()
        cots.append(c)

    upd_sum = upd_own[me]
    for k in range(n - 1):
        updates[k].wait_recv()
        upd_sum = upd_sum + upd_recv[k].astype(F32)
    cot_sum = cot_own[me]
    for k in range(n - 1):
        cots[k].wait_recv()
        cot_sum = cot_sum + cot_recv[k].astype(F32)
    total = jnp.concatenate([cot_sum, upd_sum], axis=1)
    pair_send[...] = total
    c = pltpu.make_async_remote_copy(
        src_ref=pair_send,
        dst_ref=pair_recv,
        send_sem=p_send,
        recv_sem=p_recv,
        device_id={"feat": other},
        device_id_type=MESH,
    )
    c.start()
    c.wait_recv()
    total = total + pair_recv[...]
    upd_v[0] = jnp.concatenate([total[:atoms, width:], total[atoms:, width:]], axis=1).astype(BF16)
    grad_v[0] = total[:atoms, :width]
    hvp_v[0] = total[atoms:, :width]
    stores = [
        pltpu.make_async_copy(v, hbm, store_sem.at[i])
        for i, (v, hbm) in enumerate(((upd_v, upd_hbm), (grad_v, grad_hbm), (hvp_v, hvp_hbm)))
    ]
    for s in stores:
        s.start()
    c.wait_send()
    for c in gathers + updates + cots:
        c.wait_send()
    for s in stores:
        s.wait()


def write_out(upd_ref, grad_ref, hvp_ref, upd_out, grad_out, hvp_out):
    upd_out[...] = upd_ref[...]
    grad_out[...] = grad_ref[...]
    hvp_out[...] = hvp_ref[...]


def on_device(
    atom_state,
    direction,
    upstream,
    edge_state,
    edge_src,
    edge_tgt,
    edge_blocks,
    trip_in,
    trip_out,
    trip_coef,
    w_src,
    w_tgt,
    w_in,
    w_out,
):
    n = lax.axis_size("graph")
    atoms, width = atom_state.shape[1:]
    slots = edge_state.shape[1]
    hidden = w_in.shape[1]
    half = width // 2
    trips = trip_in.shape[1]
    far = pl.BlockSpec(memory_space=pltpu.HBM)
    dma = pltpu.SemaphoreType.DMA
    outs = (
        jax.ShapeDtypeStruct((1, atoms, width), BF16),
        jax.ShapeDtypeStruct((1, atoms, width), F32),
        jax.ShapeDtypeStruct((1, atoms, width), F32),
    )
    results = pl.pallas_call(
        functools.partial(kernel, n),
        name="interaction",
        out_shape=outs,
        in_specs=[far] * 14,
        out_specs=(far, far, far),
        scratch_shapes=[
            pltpu.VMEM((1, atoms, width), BF16),
            pltpu.VMEM((1, atoms, width), BF16),
            pltpu.VMEM((1, atoms, width), BF16),
            pltpu.VMEM((1, slots), jnp.int32),
            pltpu.VMEM((1, slots), jnp.int32),
            pltpu.SMEM((1, 1), jnp.int32),
            pltpu.VMEM((1, trips), jnp.int32),
            pltpu.VMEM((1, trips), jnp.int32),
            pltpu.VMEM((1, trips), BF16),
            pltpu.VMEM((slots, width), BF16),
            pltpu.VMEM((width, width), BF16),
            pltpu.VMEM((width, width), BF16),
            pltpu.VMEM((width, hidden), BF16),
            pltpu.VMEM((hidden, width), BF16),
            pltpu.VMEM((2 * atoms, width + half), BF16),
            pltpu.VMEM((n, 2 * atoms, width + half), BF16),
            pltpu.VMEM((n, 2 * atoms, half), F32),
            pltpu.VMEM((n, 2 * atoms, half), BF16),
            pltpu.VMEM((n - 1, 2 * atoms, half), BF16),
            pltpu.VMEM((n, 2 * atoms, width), F32),
            pltpu.VMEM((n, 2 * atoms, width), BF16),
            pltpu.VMEM((n - 1, 2 * atoms, width), BF16),
            pltpu.VMEM((2 * atoms, width + half), F32),
            pltpu.VMEM((2 * atoms, width + half), F32),
            dma((14,)),
            dma((n - 1,)),
            dma((n - 1,)),
            dma((n - 1,)),
            dma((n - 1,)),
            dma((n - 1,)),
            dma((n - 1,)),
            dma,
            dma,
        ]
        + [pltpu.VMEM(o.shape, o.dtype) for o in outs]
        + [dma((3,))],
        compiler_params=pltpu.CompilerParams(
            collective_id=0, has_side_effects=True, vmem_limit_bytes=64 * 1024 * 1024
        ),
    )(
        atom_state,
        direction,
        upstream,
        edge_src,
        edge_tgt,
        edge_blocks,
        trip_in,
        trip_out,
        trip_coef,
        edge_state,
        w_src,
        w_tgt,
        w_in,
        w_out,
    )
    return pl.pallas_call(
        write_out,
        name="write_out",
        out_shape=outs,
        compiler_params=pltpu.CompilerParams(vmem_limit_bytes=64 * 1024 * 1024),
    )(*results)


def solution(mesh):
    in_specs = (
        P(("groups", "pipe"), "graph", None),
        P(("groups", "pipe"), "graph", None),
        P(("groups", "pipe"), "graph", None),
        P(("groups", "pipe"), "graph", None),
        P(("groups", "pipe"), "graph"),
        P(("groups", "pipe"), "graph"),
        P(("groups", "pipe"), "graph"),
        P(("groups", "pipe"), "graph"),
        P(("groups", "pipe"), "graph"),
        P(("groups", "pipe"), "graph"),
        P(),
        P(),
        P(None, "feat"),
        P("feat", None),
    )
    out_specs = (
        P(("groups", "pipe"), "graph", None),
        P(("groups", "pipe"), "graph", None),
        P(("groups", "pipe"), "graph", None),
    )
    return jax.shard_map(
        on_device, mesh=mesh, in_specs=in_specs, out_specs=out_specs, check_vma=False
    )
```
